32 devices in a mesh: groups: 2 (over x), samp: 16 (over z, y, core).
Axes of the slice: x: 2, y: 2, z: 4, core: 2. Of those that a mesh axis runs over, the one named last changes fastest.
Arguments:
- gradients: bfloat16 [8192, 32768], P(('groups', 'samp')), parts along dimension 0, may hold values from -45 to 45
- sketch: bfloat16 [8192, 128], P(('groups', 'samp')), parts along dimension 0, may hold values from -6 to 6
Outputs:
- basis: float32 [32768, 256], P('samp', 'groups'), parts along dimension 1
- factor: float32 [256, 128], P('groups'), parts along dimension 0
The draws below stay inside these ranges and needn't reach their ends.
There are 2 independent parts, one for each index of `groups`. The reference program is written for one: setup_inputs(seed, part) draws one part's arguments, and reference() takes and returns one part's arrays. A program takes and returns all parts, laid end to end along the dimension named above; each array names one. Nothing has to cross between parts.
All inputs are finite; a program needn't handle non-finite values.
Results may differ from the reference program's by a relative error of at most 0.0029.
Values may be sent and summed in bfloat16 or wider, within the bound.
A program may use at most 128 MiB of HBM per device.

```python
import math
import jax
import jax.numpy as jnp
from jax import lax

P_SIZE = 32768
K = 128
SAMPLES = 4096


def draw_gradients(key, part):
    key_base = jax.random.fold_in(key, 11)
    key_rows = jax.random.fold_in(key, 12)
    key_cols = jax.random.fold_in(key, 13)
    base = jnp.clip(jax.random.normal(key_base, (SAMPLES, P_SIZE), jnp.float32), -5.0, 5.0)
    row_scale = jnp.exp(jax.random.uniform(key_rows, (SAMPLES, 1), jnp.float32, math.log(0.3), math.log(3.0)))
    trend = 1.0 + 2.0 * jnp.arange(P_SIZE, dtype=jnp.float32)[None, :] / P_SIZE
    col_scale = jnp.exp(jax.random.uniform(key_cols, (1, P_SIZE), jnp.float32, math.log(0.1), 0.0)) * trend
    return (base * row_scale * col_scale).astype(jnp.bfloat16)


def block_levels(own_key, extent, cuts, low, top_value):
    level = 1.0
    for axis_at, parts in cuts:
        heights = jax.random.uniform(jax.random.fold_in(jax.random.fold_in(own_key, 6), axis_at), (parts,), jnp.float32, low / len(cuts), top_value / len(cuts))
        level = level * jnp.repeat(jnp.exp(heights), extent[axis_at] // parts).reshape((-1,) + (1,) * (len(extent) - 1 - axis_at))
    return level


def scatter_about(own_key, shape, width, most, shards=(), held_as=jnp.bfloat16):
    values = jax.random.normal(own_key, shape, jnp.float32) * width
    if len(shards) > 0:
        values = block_levels(own_key, shape, shards, -0.22, 0.18) * values
    return jnp.clip(values, min=-most, max=most).astype(held_as)


def setup_inputs(seed: int = 0, part: int = 0) -> dict:
    splits = jax.random.split(jax.random.key(seed), 3)
    own_keys = jax.random.split(jax.random.fold_in(splits[2], part), 3)
    gradients = draw_gradients(jax.random.fold_in(jax.random.fold_in(splits[2], part), 71), part)
    sketch = scatter_about(own_keys[1], (SAMPLES, K), 1.0, 6.0, ((0, 16),))
    return {"gradients": gradients, "sketch": sketch}


def block_sums(gradients, right, scale):
    term = lax.dot_general(gradients.astype(jnp.float32), right.astype(jnp.float32), (((0,), (0,)), ((), ())), preferred_element_type=jnp.float32)
    return term * scale

def orthonormal(matrix):
    gram = jnp.dot(matrix.T, matrix, precision=lax.Precision.HIGHEST) / P_SIZE
    lower = jnp.linalg.cholesky(gram)
    identity = jnp.eye(K, dtype=gram.dtype)
    inverse = lax.linalg.triangular_solve(lower, identity, left_side=True, lower=True)
    return (jnp.dot(matrix, inverse.T, precision=lax.Precision.HIGHEST), lower)

def reference(gradients, sketch):
    first = block_sums(gradients, sketch, 1.0)
    basis_one, unused = orthonormal(first)
    basis_one = basis_one.astype(jnp.bfloat16)
    image = jnp.dot(gradients.astype(jnp.float32), basis_one.astype(jnp.float32), preferred_element_type=jnp.float32).astype(jnp.bfloat16)
    second = block_sums(gradients, image, 1.0 / SAMPLES)
    basis, lower = orthonormal(second)
    return (basis, lower.T)
```

```python
import functools

import jax
import jax.numpy as jnp
from jax import lax
from jax.experimental import pallas as pl
from jax.experimental.pallas import tpu as pltpu
from jax.sharding import PartitionSpec as P

MESH = pl.DeviceIdType.MESH
SUB = 2
MIB = 1024 * 1024


def position(nz):
    me = lax.axis_index("samp")
    return lax.div(me, 4), lax.rem(lax.div(me, 2), 2), lax.rem(me, 2)


def place(z, y, c):
    return (lax.axis_index("groups"), z * 4 + y * 2 + c)


def outward(nz, z, k):
    mirror = z >= nz - z
    zm = jnp.where(mirror, nz - 1 - z, z)
    base = nz - 1 - 2 * zm
    kk = jnp.maximum(k - base, 0)
    half = lax.div(kk, 2)
    inner = jnp.where(lax.rem(kk, 2) == 0, half, 2 * zm - half)
    at = jnp.where(k < base, nz - 1 - k, inner)
    return jnp.where(mirror, nz - 1 - at, at)


def enter(nz, z, y, c):
    barrier = pltpu.get_barrier_semaphore()
    pl.semaphore_signal(barrier, inc=1, device_id=place(z, y, 1 - c), device_id_type=MESH)
    pl.semaphore_signal(barrier, inc=1, device_id=place(z, 1 - y, c), device_id_type=MESH)
    for o in range(1, nz):
        pl.semaphore_signal(
            barrier, inc=1, device_id=place(lax.rem(z + o, nz), y, c), device_id_type=MESH
        )
    pl.semaphore_wait(barrier, nz + 1)


def remote(src, dst, send, recv, to):
    return pltpu.make_async_remote_copy(
        src_ref=src, dst_ref=dst, send_sem=send, recv_sem=recv, device_id=to, device_id_type=MESH
    )


def product(own_lhs, other_lhs, own, other, idx):
    return jnp.dot(own_lhs, own[idx], preferred_element_type=jnp.float32) + jnp.dot(
        other_lhs, other[idx], preferred_element_type=jnp.float32
    )


def reduce_scatter(nz, z, y, c, partial, acc, ysend, yrecv, zsend, zrecv, sems, wide=None):
    ys, yr, zs, zr = sems

    @pl.loop(0, nz * SUB)
    def send_pair(t):
        k, h = lax.div(t, SUB), lax.rem(t, SUB)
        zd = outward(nz, z, k)
        slot = zd * SUB + h
        ysend[slot] = partial((zd * 2 + 1 - y) * SUB + h).astype(jnp.bfloat16)
        remote(
            ysend.at[slot], yrecv.at[slot], ys.at[slot], yr.at[slot], place(z, 1 - y, c)
        ).start()

    def y_copy(slot):
        return remote(
            ysend.at[slot], yrecv.at[slot], ys.at[slot], yr.at[slot], place(z, 1 - y, c)
        )

    def z_copy(slot, into, to):
        return remote(zsend.at[slot], zrecv.at[into], zs.at[slot], zr.at[into], place(to, y, c))

    def w_copy(slot, to):
        return remote(
            wide[0].at[slot], wide[1].at[slot], wide[2].at[slot], wide[3].at[slot],
            place(to, y, c),
        )

    @pl.loop(0, nz * SUB)
    def along(t):
        k, h = lax.div(t, SUB), lax.rem(t, SUB)
        zd = outward(nz, z, k)
        slot = zd * SUB + h
        acc[h] = partial((zd * 2 + y) * SUB + h)
        y_copy(slot).wait_recv()
        acc[h] += yrecv[slot].astype(jnp.float32)

        from_left_wide = jnp.logical_and(zd == z, z > 1)
        from_right_wide = jnp.logical_and(zd == z, z < nz - 2)
        to_right_wide = jnp.logical_and(zd == z + 1, z > 0)
        to_left_wide = jnp.logical_and(zd == z - 1, z < nz - 1)
        from_left, from_right = jnp.logical_and(zd >= z, z > 0), jnp.logical_and(zd <= z, z < nz - 1)
        to_right, to_left = zd > z, zd < z
        if wide is not None:
            for side, arrives in enumerate((from_left_wide, from_right_wide)):

                @pl.when(arrives)
                def take_wide():
                    w_copy(side * SUB + h, z).wait_recv()
                    acc[h] += wide[1][side * SUB + h]

            from_left = jnp.logical_and(from_left, jnp.logical_not(from_left_wide))
            from_right = jnp.logical_and(from_right, jnp.logical_not(from_right_wide))
            to_right = jnp.logical_and(to_right, jnp.logical_not(to_right_wide))
            to_left = jnp.logical_and(to_left, jnp.logical_not(to_left_wide))

        @pl.when(from_left)
        def take_left():
            z_copy(slot, slot, z).wait_recv()
            acc[h] += zrecv[slot].astype(jnp.float32)

        right = jnp.where(zd == z, nz, zd) * SUB + h

        @pl.when(from_right)
        def take_right():
            z_copy(slot, right, z).wait_recv()
            acc[h] += zrecv[right].astype(jnp.float32)

        if wide is not None:
            for side, (leaves, to) in enumerate(((to_right_wide, z + 1), (to_left_wide, z - 1))):

                @pl.when(leaves)
                def give_wide():
                    wide[0][side * SUB + h] = acc[h]
                    w_copy(side * SUB + h, to).start()

        @pl.when(to_right)
        def give_right():
            zsend[slot] = acc[h].astype(jnp.bfloat16)
            z_copy(slot, slot, z + 1).start()

        @pl.when(to_left)
        def give_left():
            zsend[slot] = acc[h].astype(jnp.bfloat16)
            z_copy(slot, jnp.where(zd == z - 1, nz, zd) * SUB + h, z - 1).start()

    @pl.loop(0, nz * SUB)
    def sent(t):
        y_copy(t).wait_send()

        zd, h = lax.div(t, SUB), lax.rem(t, SUB)
        narrow = zd != z
        if wide is not None:
            for side, zw in enumerate((z + 1, z - 1)):
                leaves = jnp.logical_and(zd == zw, (z > 0) if side == 0 else (z < nz - 1))

                @pl.when(leaves)
                def wide_sent():
                    w_copy(side * SUB + h, z).wait_send()

                narrow = jnp.logical_and(narrow, jnp.logical_not(leaves))

        @pl.when(narrow)
        def line_sent():
            z_copy(t, t, z).wait_send()


def first_kernel(
    nz, g_ref, s_ref, img_ref, gram_ref, keep_ref,
    own, other, s_other, acc, ysend, yrecv, zsend, zrecv, full, give, take,
    ys, yr, zs, zr, load, gs, gr, store, ss, ar, al, ay, arz, ary, xs,
):
    z, y, c = position(nz)
    width = own.shape[2]
    enter(nz, z, y, c)
    sibling = place(z, y, 1 - c)

    def columns(idx, core):
        p, h = lax.div(idx, SUB), lax.rem(idx, SUB)
        return pl.ds(pl.multiple_of(((p * 2 + core) * SUB + h) * width, width), width)

    def mine(idx):
        return pltpu.make_async_copy(g_ref.at[:, columns(idx, c)], own.at[idx], load.at[idx])

    def swap(idx):
        return remote(
            g_ref.at[:, columns(idx, 1 - c)], other.at[idx], gs.at[idx], gr.at[idx], sibling
        )

    def put(idx):
        return pltpu.make_async_copy(other.at[idx], keep_ref.at[idx], store.at[idx])

    sketch_copy = remote(s_ref, s_other, ss.at[0], ss.at[1], sibling)
    sketch_copy.start()
    for pair in (1, 0):

        @pl.loop(0, nz * SUB)
        def begin(t):
            zd = outward(nz, z, lax.div(t, SUB))
            yd = 1 - y if pair else y
            idx = (zd * 2 + yd) * SUB + lax.rem(t, SUB)
            swap(idx).start()
            mine(idx).start()

    sketch_copy.wait()

    def partial(idx):
        mine(idx).wait()
        swap(idx).wait_recv()
        put(idx).start()
        return product(s_ref[...], s_other[...], own, other, idx)

    reduce_scatter(nz, z, y, c, partial, acc, ysend, yrecv, zsend, zrecv, (ys, yr, zs, zr))

    give[...] = jnp.zeros_like(give)

    def block(zz, yy, h):
        return full.at[(zz * 2 + yy) * SUB + h]

    def g_right(zz, h):
        s = zz * SUB + h
        return remote(block(zz, y, h), block(zz, y, h), ar.at[s], arz.at[s], place(z + 1, y, c))

    def g_left(zz, h):
        s = zz * SUB + h
        return remote(block(zz, y, h), block(zz, y, h), al.at[s], arz.at[s], place(z - 1, y, c))

    def g_pair(zz, h):
        s = zz * SUB + h
        return remote(block(zz, y, h), block(zz, y, h), ay.at[s], ary.at[s], place(z, 1 - y, c))

    def from_pair(zz, h):
        s = zz * SUB + h
        return remote(
            block(zz, 1 - y, h), block(zz, 1 - y, h), ay.at[s], ary.at[s], place(z, 1 - y, c)
        )

    def use(idx):
        got = full[idx]
        rows = own.shape[1]
        give[:, rows : 2 * rows] += lax.dot_general(
            got, own[idx], (((1,), (1,)), ((), ())), preferred_element_type=jnp.float32
        )
        give[:, 0:rows] += lax.dot_general(
            got, other[idx], (((1,), (1,)), ((), ())), preferred_element_type=jnp.float32
        )
        give[:, 2 * rows :] += lax.dot_general(
            got, got, (((1,), (1,)), ((), ())), preferred_element_type=jnp.float32
        )

    def goes_right(zz):
        return jnp.logical_and(zz <= z, z < nz - 1)

    def goes_left(zz):
        return jnp.logical_and(zz >= z, z > 0)

    @pl.loop(0, nz * SUB)
    def line(t):
        k, h = lax.div(t, SUB), lax.rem(t, SUB)
        zz = outward(nz, z, nz - 1 - k)

        @pl.when(k == 0)
        def local():
            full[(z * 2 + y) * SUB + h] = acc[h].astype(jnp.bfloat16)

        @pl.when(k > 0)
        def arrived():
            g_right(zz, h).wait_recv()

        @pl.when(goes_right(zz))
        def right():
            g_right(zz, h).start()

        @pl.when(goes_left(zz))
        def left():
            g_left(zz, h).start()

        g_pair(zz, h).start()
        use((zz * 2 + y) * SUB + h)

    @pl.loop(0, nz * SUB)
    def pair_blocks(t):
        k, h = lax.div(t, SUB), lax.rem(t, SUB)
        zz = outward(nz, z, nz - 1 - k)
        from_pair(zz, h).wait_recv()
        use((zz * 2 + 1 - y) * SUB + h)

    exchange = remote(give, take, xs.at[0], xs.at[1], sibling)
    exchange.start()

    @pl.loop(0, nz * SUB)
    def sent(t):
        zz, h = lax.div(t, SUB), lax.rem(t, SUB)
        g_pair(zz, h).wait_send()

        @pl.when(goes_right(zz))
        def right():
            g_right(zz, h).wait_send()

        @pl.when(goes_left(zz))
        def left():
            g_left(zz, h).wait_send()

    @pl.loop(0, 2 * nz * SUB)
    def stored(t):
        put(t).wait()
        swap(t).wait_send()

    exchange.wait()
    rows = own.shape[1]
    img_ref[0] = give[:, rows : 2 * rows] + take[:, 0:rows]
    img_ref[1] = give[:, 0:rows] + take[:, rows : 2 * rows]
    gram_ref[...] = give[:, 2 * rows :] + take[:, 2 * rows :]


def second_kernel(
    nz, scale, inv_p, g_ref, keep_ref, img_ref, inv_ref, second_ref, gram_ref,
    own, other, image, acc, ysend, yrecv, zsend, zrecv, part, pair_in, line_in,
    wsend, wrecv, ys, yr, zs, zr, load, fetch, xs, vs, ws, wr,
):
    z, y, c = position(nz)
    width = own.shape[2]

    def mine(idx):
        p, h = lax.div(idx, SUB), lax.rem(idx, SUB)
        at = pl.ds(pl.multiple_of(((p * 2 + c) * SUB + h) * width, width), width)
        return pltpu.make_async_copy(g_ref.at[:, at], own.at[idx], load.at[idx])

    def kept(idx):
        return pltpu.make_async_copy(keep_ref.at[idx], other.at[idx], fetch.at[idx])

    for pair in (1, 0):

        @pl.loop(0, nz * SUB)
        def begin(t):
            zd = outward(nz, z, lax.div(t, SUB))
            yd = 1 - y if pair else y
            idx = (zd * 2 + yd) * SUB + lax.rem(t, SUB)
            mine(idx).start()
            kept(idx).start()

    enter(nz, z, y, c)
    for side in range(2):
        image[side] = jnp.dot(
            inv_ref[...], img_ref[side],
            precision=lax.Precision.HIGHEST, preferred_element_type=jnp.float32,
        ).astype(jnp.bfloat16)

    def partial(idx):
        mine(idx).wait()
        kept(idx).wait()
        return product(image[0], image[1], own, other, idx)

    reduce_scatter(
        nz, z, y, c, partial, acc, ysend, yrecv, zsend, zrecv, (ys, yr, zs, zr),
        (wsend, wrecv, ws, wr),
    )
    total = jnp.zeros(part.shape[1:], jnp.float32)
    for h in range(SUB):
        rows = acc[h] * scale
        second_ref[:, h * width : (h + 1) * width] = rows
        total = total + lax.dot_general(
            rows, rows, (((1,), (1,)), ((), ())),
            precision=lax.Precision.HIGHEST, preferred_element_type=jnp.float32,
        )
    part[0] = total * inv_p
    core = remote(part.at[0], pair_in.at[0], xs.at[0], xs.at[1], place(z, y, 1 - c))
    core.start()
    core.wait()
    part[1] = part[0] + pair_in[0]
    across = remote(part.at[1], pair_in.at[1], xs.at[2], xs.at[3], place(z, 1 - y, c))
    across.start()
    across.wait()
    part[2] = part[1] + pair_in[1]

    def line(o):
        return remote(
            part.at[2], line_in.at[o], vs.at[o], vs.at[nz + o], place(lax.rem(z + o, nz), y, c)
        )

    for o in range(1, nz):
        line(o).start()
    line_in[0] = part[2]
    for o in range(1, nz):
        line(o).wait()
    total = jnp.zeros(part.shape[1:], jnp.float32)
    for at in range(nz):
        total = total + line_in[lax.rem(z - at + nz, nz)]
    gram_ref[...] = total


def invert(gram):
    lower = jnp.linalg.cholesky(gram)
    identity = jnp.eye(gram.shape[0], dtype=jnp.float32)
    return lower, lax.linalg.triangular_solve(lower, identity, left_side=True, lower=True)


def per_device(gradients, sketch):
    rows, params = gradients.shape
    cols = sketch.shape[1]
    n = lax.axis_size("samp")
    nz = n // 4
    share = params // n
    width = share // SUB
    blocks = 2 * nz * SUB
    line = nz * SUB
    f32, bf16 = jnp.float32, jnp.bfloat16
    anywhere = pl.BlockSpec(memory_space=pl.ANY)
    vmem = pl.BlockSpec(memory_space=pltpu.VMEM)
    dma = pltpu.SemaphoreType.DMA
    limit = 48 * MIB
    reduce_buffers = [
        pltpu.VMEM((SUB, cols, width), f32),
        pltpu.VMEM((line, cols, width), bf16),
        pltpu.VMEM((line, cols, width), bf16),
        pltpu.VMEM((line, cols, width), bf16),
        pltpu.VMEM((line + SUB, cols, width), bf16),
    ]
    reduce_sems = [dma((line,)), dma((line,)), dma((line,)), dma((line + SUB,))]
    img, gram_one, keep = pl.pallas_call(
        functools.partial(first_kernel, nz),
        out_shape=(
            jax.ShapeDtypeStruct((2, cols, rows), f32),
            jax.ShapeDtypeStruct((cols, cols), f32),
            jax.ShapeDtypeStruct((blocks, rows, width), bf16),
        ),
        in_specs=[anywhere, vmem],
        out_specs=(vmem, vmem, anywhere),
        scratch_shapes=[
            pltpu.VMEM((blocks, rows, width), bf16),
            pltpu.VMEM((blocks, rows, width), bf16),
            pltpu.VMEM((cols, rows), bf16),
            *reduce_buffers,
            pltpu.VMEM((blocks, cols, width), bf16),
            pltpu.VMEM((cols, 2 * rows + cols), f32),
            pltpu.VMEM((cols, 2 * rows + cols), f32),
            *reduce_sems,
            dma((blocks,)), dma((blocks,)), dma((blocks,)), dma((blocks,)), dma((2,)),
            dma((line,)), dma((line,)), dma((line,)), dma((line,)), dma((line,)), dma((2,)),
        ],
        compiler_params=pltpu.CompilerParams(
            collective_id=0, has_side_effects=True, vmem_limit_bytes=limit
        ),
        name="first_pass",
    )(gradients, sketch.T)
    unused, inverse_one = invert(gram_one / params)
    second, gram_two = pl.pallas_call(
        functools.partial(second_kernel, nz, 1.0 / (rows * n), 1.0 / params),
        out_shape=(
            jax.ShapeDtypeStruct((cols, share), f32),
            jax.ShapeDtypeStruct((cols, cols), f32),
        ),
        in_specs=[anywhere, anywhere, vmem, vmem],
        out_specs=(vmem, vmem),
        scratch_shapes=[
            pltpu.VMEM((blocks, rows, width), bf16),
            pltpu.VMEM((blocks, rows, width), bf16),
            pltpu.VMEM((2, cols, rows), bf16),
            *reduce_buffers,
            pltpu.VMEM((3, cols, cols), f32),
            pltpu.VMEM((2, cols, cols), f32),
            pltpu.VMEM((nz, cols, cols), f32),
            pltpu.VMEM((2 * SUB, cols, width), f32),
            pltpu.VMEM((2 * SUB, cols, width), f32),
            *reduce_sems,
            dma((blocks,)), dma((blocks,)), dma((4,)), dma((2 * nz,)), dma((2 * SUB,)), dma((2 * SUB,)),
        ],
        compiler_params=pltpu.CompilerParams(
            collective_id=1, has_side_effects=True, vmem_limit_bytes=limit
        ),
        name="second_pass",
    )(gradients, keep, img, inverse_one)
    lower, inverse_two = invert(gram_two)
    basis = lax.dot_general(
        second, inverse_two, (((0,), (1,)), ((), ())),
        precision=lax.Precision.HIGHEST, preferred_element_type=f32,
    )
    return (basis, lower.T)


def solution(mesh):
    placed = (P(("groups", "samp"), None), P(("groups", "samp"), None))
    return jax.shard_map(
        per_device,
        mesh=mesh,
        in_specs=placed,
        out_specs=(P("samp", "groups"), P("groups", None)),
        check_vma=False,
    )
```
